256 devices in a mesh: row: 8 (over x, y_lo), col: 32 (over z, y_hi, core).
Axes of the slice: x: 4, y: 4 (y_hi: 2, y_lo: 2; y = y_hi * 2 + y_lo), z: 8, core: 2. Of those that a mesh axis runs over, the one named last changes fastest.
Arguments:
- activations: bfloat16 [2048, 6144], P('row', 'col'), may hold values from -600 to 600
- norm_gain: bfloat16 [6144], P('col'), may hold values from 0.099609375 to 1.8984375
- in_weight: bfloat16 [6144, 24576], P('row', 'col'), may hold values from -0.078125 to 0.078125
- in_bias: float32 [24576], P('col'), may hold values from -3 to 3
- out_cotangent: bfloat16 [2048, 24576], P('row', 'col'), may hold values from -6 to 6
Outputs:
- hidden: bfloat16 [2048, 24576], P('row', 'col')
- input_grad: bfloat16 [2048, 6144], P('row', 'col')
- weight_grad: float32 [6144, 24576], P('row', 'col')
- bias_grad: float32 [24576], P('col')
- gain_grad: float32 [6144], P('col')
The draws below stay inside these ranges and needn't reach their ends.
All inputs are finite; a program needn't handle non-finite values.
Results may differ from the reference program's by a relative error of at most 0.023.
Values may be sent and summed in bfloat16 or wider, within the bound.
No kernel may reach another device: no remote copies, remote signals or barrier semaphores. Data moves between devices by JAX's collectives and lax.ppermute only.
A program may use at most 128 MiB of HBM per device.

```python
import math
import jax
import jax.numpy as jnp
from jax import lax

D = 6144
FF = 24576
TOKENS = 2048


def draw_activations(key, part):
    key = jax.random.fold_in(key, 1)
    base_key, col_key, row_key = jax.random.split(key, 3)
    col_scale = jnp.exp(jax.random.uniform(col_key, (D,), jnp.float32, -1.15, 1.15))
    col_scale = col_scale * 3.0 ** (jnp.arange(D, dtype=jnp.float32) / D)
    row_scale = jnp.exp(jax.random.uniform(row_key, (TOKENS, 1), jnp.float32, 0.0, 2.3))
    base = jnp.clip(jax.random.normal(base_key, (TOKENS, D), jnp.float32), -6.0, 6.0)
    return (base * row_scale * col_scale[None, :]).astype(jnp.bfloat16)


def block_scale(stream_key, shape, pieces, low, largest):
    def one(position, blocks):
        draws = jax.random.uniform(jax.random.fold_in(jax.random.fold_in(stream_key, 6), position), (blocks,), jnp.float32, low / len(pieces), largest / len(pieces))
        return jnp.repeat(jnp.exp(draws), shape[position] // blocks).reshape((-1,) + (1,) * (len(shape) - position - 1))

    gain = one(*pieces[0])
    for cut in pieces[1:]:
        gain = gain * one(*cut)
    return gain


def centred(rng, shape, deviation, reach, cuts=(), kind=jnp.bfloat16):
    entries = deviation * jax.random.normal(rng, shape, jnp.float32)
    if cuts:
        entries = entries * block_scale(rng, shape, cuts, -0.22, 0.18)
    return jnp.clip(entries, -reach, reach).astype(kind)


def setup_inputs(seed: int = 0) -> dict:
    key_list = jax.random.split(jax.random.key(seed), 6)
    return {
        "activations": draw_activations(jax.random.fold_in(key_list[5], 71), 0),
        "norm_gain": jnp.clip(1.0 + 0.18 * jax.random.normal(key_list[1], (D,), jnp.float32), 0.099609375, 1.8984375).astype(jnp.bfloat16),
        "in_weight": centred(key_list[2], (D, FF), D ** -0.5, 0.078125, ((0, 8), (1, 32))),
        "in_bias": centred(key_list[3], (FF,), 0.5, 3.0, ((0, 32),), jnp.float32),
        "out_cotangent": centred(key_list[4], (TOKENS, FF), 1.0, 6.0, ((0, 8), (1, 32))),
    }


def gelu_parts(preact):
    coeff = math.sqrt(2.0 / math.pi)
    inner = coeff * (preact + 0.044715 * preact * preact * preact)
    tanh_val = jnp.tanh(inner)
    value = 0.5 * preact * (1.0 + tanh_val)
    slope = 0.5 * (1.0 + tanh_val) + 0.5 * preact * (1.0 - tanh_val * tanh_val) * coeff * (1.0 + 3.0 * 0.044715 * preact * preact)
    return (value, slope)

def reference(activations, norm_gain, in_weight, in_bias, out_cotangent):
    widened = activations.astype(jnp.float32)
    average = lax.optimization_barrier(jnp.sum(widened, axis=1, keepdims=True)) / D
    variance = lax.optimization_barrier(jnp.sum(widened * widened, axis=1, keepdims=True)) / D - average * average
    inv_std = lax.rsqrt(variance + 1e-06)
    x_hat = (widened - average) * inv_std
    gain_wide = norm_gain.astype(jnp.float32)
    normed = (x_hat * gain_wide).astype(jnp.bfloat16)
    preact = jnp.dot(normed, in_weight, preferred_element_type=jnp.float32) + in_bias
    value, slope = gelu_parts(preact)
    hidden = value.astype(jnp.bfloat16)
    pre_grad = (out_cotangent.astype(jnp.float32) * slope).astype(jnp.bfloat16)
    bias_grad = lax.optimization_barrier(jnp.sum(pre_grad.astype(jnp.float32), axis=0))
    weight_grad = lax.dot_general(normed, pre_grad, (((0,), (0,)), ((), ())), preferred_element_type=jnp.float32)
    normed_grad = lax.dot_general(pre_grad, in_weight, (((1,), (1,)), ((), ())), preferred_element_type=jnp.float32)
    gain_grad = lax.optimization_barrier(jnp.sum(normed_grad * x_hat, axis=0))
    scaled = normed_grad * gain_wide
    first_sum = lax.optimization_barrier(jnp.sum(scaled, axis=1, keepdims=True)) / D
    second_sum = lax.optimization_barrier(jnp.sum(scaled * x_hat, axis=1, keepdims=True)) / D
    input_grad = (inv_std * (scaled - first_sum - x_hat * second_sum)).astype(jnp.bfloat16)
    return (hidden, input_grad, weight_grad, bias_grad, gain_grad)
```

```python
import functools
import math

import jax
import jax.numpy as jnp
from jax import lax
from jax.experimental import pallas as pl
from jax.experimental.pallas import tpu as pltpu
from jax.sharding import Mesh
from jax.sharding import PartitionSpec as P

D = 6144
PANEL = 768
BLOCK = 192
HALF = 384
TOK = 256
N = 1
T = TOK // N
AXES = ("x", "yl", "z", "yh", "k")
SIZES = (4, 2, 8, 2, 2)
ROW = ("x", "yl")
COL = ("z", "yh", "k")
f32, bf16 = jnp.float32, jnp.bfloat16


def gelu_parts(preact):
    coeff = math.sqrt(2.0 / math.pi)
    inner = coeff * (preact + 0.044715 * preact * preact * preact)
    tanh_val = jnp.tanh(inner)
    value = 0.5 * preact * (1.0 + tanh_val)
    slope = 0.5 * (1.0 + tanh_val) + 0.5 * preact * (1.0 - tanh_val * tanh_val) * coeff * (
        1.0 + 3.0 * 0.044715 * preact * preact
    )
    return (value, slope)


def shift(value, axis, by):
    size = SIZES[AXES.index(axis)]
    return lax.ppermute(value, axis, [(i, (i + by) % size) for i in range(size)])


def transpose_pairs(inverse):
    pairs = []
    for r in range(8):
        for z in range(8):
            for q in range(4):
                here, there = r * 32 + z * 4 + q, z * 32 + r * 4 + q
                pairs.append((there, here) if inverse else (here, there))
    return pairs


def to_all(value, axes, count):
    return lax.all_to_all(
        jnp.broadcast_to(value[None], (count,) + value.shape), axes, 0, 0
    )


def norm_matmul_kernel(idx, own, other, stats, gain, wt, normed, partial):
    first = idx[1] == 0
    a, b = own[0].astype(f32), other[0].astype(f32)
    low, high = jnp.where(first, a, b), jnp.where(first, b, a)
    x = jnp.concatenate([low[:BLOCK], high[:BLOCK], low[BLOCK:], high[BLOCK:]], axis=0)
    average = stats[0, 0:1, :] / D
    variance = stats[0, 1:2, :] / D - average * average
    inv_std = lax.rsqrt(variance + 1e-06)
    n = ((x - average) * inv_std * gain[...]).astype(bf16)
    normed[0] = n
    partial[0] = jnp.dot(wt[...], n, preferred_element_type=f32).astype(bf16)


def norm_matmul(idx, own, other, stats, gain, wt):
    blk = pl.BlockSpec((1, HALF, T), lambda p, s: ((s[0] + 8 - p) % 8, 0, 0))
    out = pl.BlockSpec((1, PANEL, T), lambda p, s: (p, 0, 0))
    return pl.pallas_call(
        norm_matmul_kernel,
        grid_spec=pltpu.PrefetchScalarGridSpec(
            num_scalar_prefetch=1,
            grid=(8,),
            in_specs=[
                blk,
                blk,
                pl.BlockSpec((1, 2, T), lambda p, s: (p, 0, 0)),
                pl.BlockSpec((PANEL, 1), lambda p, s: (0, 0)),
                pl.BlockSpec((PANEL, PANEL), lambda p, s: (0, 0)),
            ],
            out_specs=[out, out],
        ),
        out_shape=[jax.ShapeDtypeStruct((8, PANEL, T), bf16)] * 2,
        compiler_params=pltpu.CompilerParams(vmem_limit_bytes=32 * 2**20),
        cost_estimate=pl.CostEstimate(
            flops=2 * 8 * PANEL * PANEL * T, bytes_accessed=10_000_000, transcendentals=0
        ),
        name="norm_matmul",
    )(idx, own, other, stats, gain, wt)


def back_matmul_kernel(idx, w, grad, mine, theirs):
    first = idx[1] == 0
    dx = jnp.dot(w[...], grad[0], preferred_element_type=f32)
    low = jnp.concatenate([dx[:BLOCK], dx[2 * BLOCK : 3 * BLOCK]], axis=0)
    high = jnp.concatenate([dx[BLOCK : 2 * BLOCK], dx[3 * BLOCK :]], axis=0)
    mine[0] = jnp.where(first, low, high).astype(bf16)
    theirs[0] = jnp.where(first, high, low).astype(bf16)


def back_matmul(idx, w, grad):
    out = pl.BlockSpec((1, HALF, T), lambda p, s: (p, 0, 0))
    return pl.pallas_call(
        back_matmul_kernel,
        grid_spec=pltpu.PrefetchScalarGridSpec(
            num_scalar_prefetch=1,
            grid=(8,),
            in_specs=[
                pl.BlockSpec((PANEL, PANEL), lambda p, s: (0, 0)),
                pl.BlockSpec((1, PANEL, T), lambda p, s: (p, 0, 0)),
            ],
            out_specs=[out, out],
        ),
        out_shape=[jax.ShapeDtypeStruct((8, HALF, T), bf16)] * 2,
        compiler_params=pltpu.CompilerParams(vmem_limit_bytes=32 * 2**20),
        cost_estimate=pl.CostEstimate(
            flops=2 * 8 * PANEL * PANEL * T, bytes_accessed=8_000_000, transcendentals=0
        ),
        name="back_matmul",
    )(idx, w, grad)


def weight_grad_kernel(*refs):
    normed, grads = refs[:N], refs[N : 2 * N]
    w, out, bias, rows = refs[2 * N :]
    step = pl.program_id(0)

    @pl.when(step == 0)
    def _():
        out[...] = jnp.zeros_like(out)
        bias[...] = jnp.zeros_like(bias)

    total = out[...]
    bias_total = bias[...]
    for n, g in zip(normed, grads):
        total = total + lax.dot_general(
            n[0], g[0], (((1,), (1,)), ((), ())), preferred_element_type=f32
        )
        bias_total = bias_total + jnp.sum(g[0].astype(f32), axis=1, keepdims=True)
    out[...] = total
    bias[...] = bias_total

    @pl.when(step == 7)
    def _():
        rows[...] = jnp.sum(out[...] * w[...].astype(f32), axis=1, keepdims=True)


def weight_grads(normed, grads, w):
    blk = pl.BlockSpec((1, PANEL, T), lambda p: (p, 0, 0))
    whole = pl.BlockSpec((PANEL, PANEL), lambda p: (0, 0))
    column = pl.BlockSpec((PANEL, 1), lambda p: (0, 0))
    return pl.pallas_call(
        weight_grad_kernel,
        grid=(8,),
        in_specs=[blk] * (2 * N) + [whole],
        out_specs=[whole, column, column],
        out_shape=[
            jax.ShapeDtypeStruct((PANEL, PANEL), f32),
            jax.ShapeDtypeStruct((PANEL, 1), f32),
            jax.ShapeDtypeStruct((PANEL, 1), f32),
        ],
        compiler_params=pltpu.CompilerParams(vmem_limit_bytes=32 * 2**20),
        cost_estimate=pl.CostEstimate(
            flops=2 * 8 * N * PANEL * PANEL * T, bytes_accessed=10_000_000, transcendentals=0
        ),
        name="weight_grads",
    )(*normed, *grads, w)


def pick(stack, index):
    return lax.dynamic_index_in_dim(stack, index, 0, keepdims=False)


def gather_z(block):
    up = down = block
    got = {0: block}
    for step in range(1, 5):
        up = shift(up, "z", 1)
        got[step] = up
        if step < 4:
            down = shift(down, "z", -1)
            got[8 - step] = down
    return jnp.stack([got[j] for j in range(8)])


def scatter_z(mine, other, z):
    def term(offset):
        i = (z + offset + 8) % 8
        return pick(mine, i).astype(f32) + pick(other, i).astype(f32)

    up, down = term(4).astype(bf16), term(-3).astype(bf16)
    for step in range(1, 4):
        up = shift(up, "z", 1)
        up = (up.astype(f32) + term(4 - step)).astype(bf16)
        down = shift(down, "z", -1)
        if step < 3:
            down = (down.astype(f32) + term(step - 3)).astype(bf16)
    up = shift(up, "z", 1)
    return up.astype(f32) + down.astype(f32) + term(0)


def per_device(activations, norm_gain, in_weight, in_bias, out_cotangent):
    row = lax.axis_index(ROW)
    col = lax.axis_index(COL)
    z, yh, k = lax.axis_index("z"), lax.axis_index("yh"), lax.axis_index("k")
    idx = jnp.stack([z, k]).astype(jnp.int32)

    act_t = activations.T
    wide_t = act_t.astype(f32)
    gain_own = norm_gain.astype(f32)

    parts = jnp.stack([act_t[:, i * T : (i + 1) * T] for i in range(N)])
    parts = lax.ppermute(parts, AXES, transpose_pairs(False))
    swapped = shift(parts, "yh", 1)
    parts = jnp.where(
        yh == 0,
        jnp.concatenate([parts, swapped], axis=1),
        jnp.concatenate([swapped, parts], axis=1),
    )

    small = jnp.concatenate(
        [
            jnp.sum(wide_t, axis=0),
            jnp.sum(wide_t * wide_t, axis=0),
            gain_own,
            jnp.zeros((320,), f32),
        ]
    ).reshape(8, 128)
    smalls = to_all(small, COL, 32).reshape(32, 1024)
    sums = jnp.sum(smalls[:, : 2 * TOK], axis=0)
    gain_panel = lax.dynamic_slice(smalls[:, 512:704], (4 * row, 0), (4, BLOCK)).reshape(PANEL, 1)
    w_wide = in_weight.astype(f32)
    wsum = jnp.sum(w_wide * gain_panel, axis=0)
    more = jnp.concatenate([sums, wsum, jnp.zeros((768,), f32)]).reshape(16, 128)
    mores = to_all(more, ROW, 8).reshape(8, 2048)
    wsum = jnp.sum(mores[:, 512:1280], axis=0)
    stats = mores[:, :512].reshape(8, 2, N, T)

    wt = in_weight.T
    cot_t = out_cotangent.T
    bias_col = in_bias[:, None]
    wsum_col = wsum[:, None]

    normed, hidden, grads, s1, s2 = [], [], [], [], []
    for i in range(N):
        own = gather_z(parts[i])
        other = shift(own, "k", 1)
        n, partial = norm_matmul(idx, own, other, stats[:, :, i], gain_panel, wt)
        normed.append(n)
        recv = lax.all_to_all(partial, ROW, 0, 0)
        linear = jnp.sum(recv.astype(f32), axis=0)
        value, slope = gelu_parts(linear + bias_col)
        hidden.append(value.astype(bf16))
        grad = (cot_t[:, i * T : (i + 1) * T].astype(f32) * slope).astype(bf16)
        wide = grad.astype(f32)
        s1.append(jnp.sum(wide * wsum_col, axis=0))
        s2.append(jnp.sum(wide * linear, axis=0))
        grads.append(to_all(grad, ROW, 8))

    pieces = []
    for i in range(N):
        mine, theirs = back_matmul(idx, in_weight, grads[i])
        total = scatter_z(mine, shift(theirs, "k", 1), z)
        kept = jnp.where(yh == 0, total[:BLOCK], total[BLOCK:])
        sent = jnp.where(yh == 0, total[BLOCK:], total[:BLOCK]).astype(bf16)
        kept = kept + shift(sent, "yh", 1).astype(f32)
        pieces.append(kept.astype(bf16))
    back = lax.ppermute(jnp.stack(pieces), AXES, transpose_pairs(True))
    normed_grad = jnp.concatenate([back[i] for i in range(N)], axis=1).astype(f32)

    weight_grad, bias_grad, rows = weight_grads(normed, grads, in_weight)

    pair = jnp.concatenate(s1 + s2).reshape(4, 128)
    totals = jnp.sum(to_all(pair, COL, 32), axis=0).reshape(2, 1, TOK)
    average = sums[None, :TOK] / D
    variance = sums[None, TOK:] / D - average * average
    inv_std = lax.rsqrt(variance + 1e-06)
    x_hat = (wide_t - average) * inv_std
    scaled = normed_grad * gain_own[:, None]
    input_grad = (inv_std * (scaled - totals[0] / D - x_hat * totals[1] / D)).astype(bf16).T

    rows = jnp.concatenate([rows[:, 0], jnp.zeros((256,), f32)]).reshape(8, 128)
    rows = jnp.sum(to_all(rows, COL, 32), axis=0)
    rows = to_all(rows, ROW, 8).reshape(8, 1024)[:, :PANEL].reshape(32, BLOCK)
    gain_grad = pick(rows, col) / gain_own

    hidden = jnp.concatenate(hidden, axis=1).T
    return (hidden, input_grad, weight_grad, bias_grad[:, 0], gain_grad)


def solution(mesh):
    fine = Mesh(mesh.devices.reshape(SIZES), AXES)
    both = P(ROW, COL)
    return jax.shard_map(
        per_device,
        mesh=fine,
        in_specs=(both, P(COL), both, P(COL), both),
        out_specs=(both, both, both, P(COL), P(COL)),
        check_vma=False,
    )
```

```python
import math

import jax
import jax.numpy as jnp
from jax import lax
from jax.experimental import pallas as pl
from jax.experimental.pallas import tpu as pltpu
from jax.sharding import Mesh
from jax.sharding import PartitionSpec as P

D = 6144
PANEL = 768
BLOCK = 192
TOK = 256
Q = 64
VMEM = 60 * 2**20
AXES = ("x", "yl", "z", "yh", "k")
SIZES = (4, 2, 8, 2, 2)
ROW = ("x", "yl")
COL = ("z", "yh", "k")
QUAD = ("yh", "k")
f32, bf16 = jnp.float32, jnp.bfloat16


def gelu_parts(preact):
    coeff = math.sqrt(2.0 / math.pi)
    inner = coeff * (preact + 0.044715 * preact * preact * preact)
    tanh_val = jnp.tanh(inner)
    value = 0.5 * preact * (1.0 + tanh_val)
    slope = 0.5 * (1.0 + tanh_val) + 0.5 * preact * (1.0 - tanh_val * tanh_val) * coeff * (
        1.0 + 3.0 * 0.044715 * preact * preact
    )
    return (value, slope)


def shift(value, axis, by):
    size = SIZES[AXES.index(axis)]
    return lax.ppermute(value, axis, [(i, (i + by) % size) for i in range(size)])


def swap(value, m):
    return lax.ppermute(value, QUAD, [(i, i ^ m) for i in range(4)]) if m else value


def transpose(value):
    pairs = []
    for r in range(8):
        for z in range(8):
            for q in range(4):
                pairs.append((r * 32 + z * 4 + q, z * 32 + r * 4 + q))
    return lax.ppermute(value, AXES, pairs)


def to_all(value, axes, count):
    return lax.all_to_all(
        jnp.broadcast_to(value[None], (count,) + value.shape), axes, 0, 0
    )


def pick(stack, index):
    return lax.dynamic_index_in_dim(stack, index, 0, keepdims=False)


def trade(stack, q):
    got = jnp.stack([swap(pick(stack, q ^ m), m) for m in range(4)])
    return [pick(got, q ^ i) for i in range(4)]


def in_three(value):
    high = lax.reduce_precision(value, 8, 7)
    middle = lax.reduce_precision(value - high, 8, 7)
    return jnp.concatenate([high, middle, value - high - middle]).astype(bf16)


def padded(rows, count=16):
    return jnp.concatenate([rows, jnp.zeros((count - rows.shape[0], rows.shape[1]), rows.dtype)])


def split(value, count):
    parts = []
    for _ in range(count):
        parts.append(value.astype(bf16).astype(f32))
        value = value - parts[-1]
    return parts


def call(kernel, name, arrays, out_shape, flops):
    vmem = pl.BlockSpec(memory_space=pltpu.VMEM)
    return pl.pallas_call(
        kernel,
        in_specs=[vmem] * len(arrays),
        out_specs=[vmem] * len(out_shape),
        out_shape=out_shape,
        compiler_params=pltpu.CompilerParams(vmem_limit_bytes=VMEM),
        cost_estimate=pl.CostEstimate(flops=flops, bytes_accessed=2**20, transcendentals=0),
        name=name,
    )(*arrays)


def streamed(kernel, name, scalars, blocked, streams, out_shape, scratch):
    vmem = pl.BlockSpec(memory_space=pltpu.VMEM)
    return pl.pallas_call(
        kernel,
        in_specs=[pl.BlockSpec(memory_space=pltpu.SMEM)]
        + [vmem] * len(blocked)
        + [pl.BlockSpec(memory_space=pl.ANY)] * len(streams),
        out_specs=[vmem] * len(out_shape),
        out_shape=out_shape,
        scratch_shapes=scratch + [pltpu.SemaphoreType.DMA((len(streams),))],
        compiler_params=pltpu.CompilerParams(vmem_limit_bytes=VMEM),
        cost_estimate=pl.CostEstimate(flops=0, bytes_accessed=2**20, transcendentals=0),
        name=name,
    )(scalars, *blocked, *streams)


W_SCRATCH = pltpu.VMEM((4, PANEL, PANEL), bf16)
G_SCRATCH = pltpu.VMEM((8 * Q, 4 * PANEL), bf16)


def row_copies(s, rows, all_rows, sems):
    copies = []
    for i in range(8):
        at = pl.ds(pl.multiple_of(s[i] * Q, Q), Q)
        copies.append(pltpu.make_async_copy(rows[i], all_rows.at[at], sems.at[i]))
    return copies


def forward_kernel(s, normed, gain, w0, w1, w2, w3, out, held, sems):
    copies = [
        pltpu.make_async_copy(w, held.at[i], sems.at[i]) for i, w in enumerate((w0, w1, w2, w3))
    ]
    for copy in copies:
        copy.start()
    sums = []
    for i in range(4):
        copies[i].wait()
        w = held[i]
        part = jnp.dot(normed[...], w, preferred_element_type=f32).astype(bf16)
        for j in range(8):
            out[j, :, i * PANEL : (i + 1) * PANEL] = part[j * Q : (j + 1) * Q]
        one = jnp.sum(w.astype(f32) * gain[...], axis=0, keepdims=True)
        sums += [one[:, j * 128 : (j + 1) * 128] for j in range(6)]
    extra = split(jnp.concatenate(sums, axis=0), 2) + [jnp.zeros((16, 128), f32)]
    extra = jnp.concatenate(extra, axis=0).astype(bf16)
    for j in range(8):
        out[j, :, 4 * PANEL :] = extra


def forward(scalars, normed, gain, ws):
    shape = jax.ShapeDtypeStruct((8, Q, 4 * PANEL + 128), bf16)
    return streamed(
        forward_kernel, "forward", scalars, [normed, gain], ws, [shape], [W_SCRATCH]
    )[0]


def backward_kernel(s, normed, pair, *refs):
    rows, ws, (out, held, grads, sems) = refs[:8], refs[8:12], refs[12:]
    copies = row_copies(s, rows, grads, sems)
    for i, w in enumerate(ws):
        copies.append(pltpu.make_async_copy(w, held.at[i], sems.at[8 + i]))
    for copy in copies:
        copy.start()
    for copy in copies[:8]:
        copy.wait()
    total = None
    for i in range(4):
        copies[8 + i].wait()
        part = lax.dot_general(
            grads[:, i * PANEL : (i + 1) * PANEL], held[i], (((1,), (1,)), ((), ())),
            preferred_element_type=f32,
        )
        total = part if total is None else total + part
    sums = jnp.sum(total * normed[...].astype(f32), axis=0, keepdims=True)
    extra = [pair[...]] + split(sums, 3) + [jnp.zeros((12, PANEL), f32)]
    extra = jnp.concatenate(extra, axis=0).astype(bf16)
    total = total.astype(bf16)
    for j in range(8):
        out[j, :Q] = total[j * Q : (j + 1) * Q]
        out[j, Q:] = extra


def backward(scalars, grads, normed, pair, ws):
    shape = jax.ShapeDtypeStruct((8, Q + 16, PANEL), bf16)
    return streamed(
        backward_kernel, "backward", scalars, [normed, pair], [*grads, *ws], [shape],
        [W_SCRATCH, G_SCRATCH],
    )[0]


def weight_kernel(s, normed, *refs):
    rows, (near, near_far, far, own, bias, grads, sems) = refs[:8], refs[8:]
    copies = row_copies(s, rows, grads, sems)
    for copy in copies:
        copy.start()
    for copy in copies:
        copy.wait()
    for i, out in ((3, near_far), (1, far), (2, near), (0, own)):
        at = slice(i * PANEL, (i + 1) * PANEL)
        out[...] = lax.dot_general(
            normed[...], grads[:, at], (((0,), (0,)), ((), ())), preferred_element_type=f32
        ).astype(out.dtype)
    bias[...] = jnp.sum(grads[...].astype(f32), axis=0, keepdims=True)


def weight_products(scalars, normed, grads):
    shapes = [
        jax.ShapeDtypeStruct((PANEL, PANEL), bf16),
        jax.ShapeDtypeStruct((PANEL, PANEL), bf16),
        jax.ShapeDtypeStruct((PANEL, PANEL), f32),
        jax.ShapeDtypeStruct((PANEL, PANEL), f32),
        jax.ShapeDtypeStruct((1, 4 * PANEL), f32),
    ]
    return streamed(
        weight_kernel, "weight_products", scalars, [normed], grads, shapes, [G_SCRATCH]
    )


def collect_kernel(parts, out, pair):
    total = parts[0].astype(f32)
    for j in range(1, 8):
        total = total + parts[j].astype(f32)
    out[:Q] = total[:Q].astype(bf16)
    pair[...] = total[Q : Q + 1]
    rows = jnp.sum(total[Q + 1 : Q + 4], axis=0, keepdims=True)
    extra = split(rows, 3) + [jnp.zeros((13, PANEL), f32)]
    out[Q:] = jnp.concatenate(extra, axis=0).astype(bf16)


def collect(parts):
    shapes = [
        jax.ShapeDtypeStruct((Q + 16, PANEL), bf16),
        jax.ShapeDtypeStruct((1, PANEL), f32),
    ]
    return call(collect_kernel, "collect", [parts], shapes, 0)


def together(*values):
    return lax.optimization_barrier(values)


def per_device(activations, norm_gain, in_weight, in_bias, out_cotangent):
    row = lax.axis_index(ROW)
    z = lax.axis_index("z")
    q = lax.axis_index(QUAD)
    order = (0, 2, 1, 3)
    px, py = lax.axis_index("x"), lax.axis_index("yl")
    around = ((0, 0), (0, 1), (3, 0), (1, 0), (3, 1), (1, 1), (2, 0), (2, 1))
    scalars = jnp.stack([(px + a) % 4 * 2 + (py + b) % 2 for a, b in around]).astype(jnp.int32)

    x = jnp.concatenate(trade(activations.reshape(4, Q, BLOCK), q), axis=1)

    wide = activations.astype(f32)
    small = jnp.concatenate(
        [
            jnp.sum(wide, axis=1),
            jnp.sum(wide * wide, axis=1),
            norm_gain.astype(f32),
            jnp.zeros((64,), f32),
            in_bias,
            jnp.zeros((512,), f32),
        ]
    ).reshape(16, 128)
    smalls = to_all(small, COL, 32).reshape(32, 2048)
    x, smalls = together(x, smalls)
    sums = jnp.sum(smalls[:, : 2 * TOK], axis=0).reshape(2, 4, Q, 1)
    sums = lax.dynamic_index_in_dim(sums, q, 1, keepdims=False)
    gains = smalls[:, 512:704]
    gain = lax.dynamic_slice(gains, (4 * z, 0), (4, BLOCK)).reshape(1, PANEL)
    average = sums[0] / D
    variance = sums[1] / D - average * average
    inv_std = lax.rsqrt(variance + 1e-06)
    x_hat = (x.astype(f32) - average) * inv_std
    normed = (x_hat * gain).astype(bf16)

    normed, weight = together(normed, in_weight)
    normed = transpose(normed)
    w_far, w_near = swap(weight, 2), swap(weight, 1)
    w_far = together(w_far, normed)[0]
    normed = to_all(normed, "z", 8).reshape(8 * Q, PANEL)
    ws = (weight, w_far, w_near, swap(w_far, 1))
    gain_row = lax.dynamic_slice(gains, (4 * row, 0), (4, BLOCK)).reshape(PANEL, 1)
    cot = out_cotangent.reshape(4, Q, PANEL)
    cot = jnp.concatenate([swap(pick(cot, q ^ m), m) for m in order], axis=1)
    normed, ws, gain_row, cot = together(normed, ws, gain_row, cot)

    recv = lax.all_to_all(forward(scalars, normed, gain_row, ws), ROW, 0, 0)
    biases = smalls[:, 768:1536]
    bias = jnp.concatenate([pick(biases, z * 4 + (q ^ m)) for m in order])
    recv, bias = together(recv, bias)
    total = jnp.sum(recv.astype(f32), axis=0)
    linear = total[:, : 4 * PANEL]
    value, slope = gelu_parts(linear + bias)
    hidden = value.astype(bf16)
    grad = (cot.astype(f32) * slope).astype(bf16)

    beside, below, above = shift(grad, "yl", 1), shift(grad, "x", 1), shift(grad, "x", -1)
    below_beside, above_beside = shift(beside, "x", 1), shift(above, "yl", 1)
    across = jnp.concatenate(
        [shift(below[: Q // 2], "x", 1), shift(above[Q // 2 :], "x", -1)], axis=0
    )
    across_beside = shift(across, "yl", 1)
    grads = [grad, beside, below, above, below_beside, above_beside, across, across_beside]
    wsum = (total[:24, 4 * PANEL :] + total[24:48, 4 * PANEL :]).reshape(1, 4 * PANEL)
    pair = jnp.concatenate(
        [jnp.sum(grad.astype(f32) * wsum, axis=1), jnp.sum(grad.astype(f32) * linear, axis=1)]
    )
    hidden, grads = together(hidden, grads)
    got = [swap(hidden[:, i * PANEL : (i + 1) * PANEL], m) for i, m in enumerate(order)]
    got = jnp.stack([got[order.index(m)] for m in range(4)])
    hidden = jnp.concatenate([pick(got, q ^ i) for i in range(4)], axis=0)
    pair = in_three(pair[None]).astype(f32).reshape(1, 384)
    pair = jnp.pad(pair, ((0, 0), (0, 384)))
    grads, pair = together(grads, pair)

    back = backward(scalars, grads, normed, pair, ws)
    back, grads, hidden = together(back, grads, hidden)
    back = lax.all_to_all(back, "z", 0, 0)
    near, near_far, far, own, bias_total = weight_products(scalars, normed, grads)
    near_far = swap(near_far, 1)
    far = (far + near_far.astype(f32)).astype(bf16)
    far = swap(far, 2)

    near = swap(near, 1)
    back, far = together(back, far)
    back, pair = collect(back)
    pair = pair[0, :384].reshape(3, 2, Q, 1)
    pair = pair[0] + pair[1] + pair[2]
    back = transpose(back)
    scaled = back[:Q].astype(f32) * gain
    input_grad = (inv_std * (scaled - pair[0] / D - x_hat * (pair[1] / D))).astype(bf16)
    input_grad = jnp.concatenate([input_grad, back[Q:]])
    input_grad = jnp.stack([input_grad[:, i * BLOCK : (i + 1) * BLOCK] for i in range(4)])
    pieces = trade(input_grad, q)
    bias_total = together(bias_total, input_grad)[0]
    bias_near = bias_total[:, : 2 * PANEL] + swap(bias_total[:, 2 * PANEL :], 1)
    bias_far = swap(bias_near[:, PANEL:], 2)
    input_grad = jnp.concatenate([p[:Q] for p in pieces], axis=0)
    rows = jnp.sum(sum(p[Q : Q + 3].astype(f32) for p in pieces), axis=0)
    gain_grad = rows / norm_gain.astype(f32)

    weight_grad = own + near.astype(f32) + far.astype(f32)
    bias_grad = (bias_near[:, :PANEL] + bias_far)[0]
    return (hidden, input_grad, weight_grad, bias_grad, gain_grad)


def solution(mesh):
    fine = Mesh(mesh.devices.reshape(SIZES), AXES)
    both = P(ROW, COL)
    return jax.shard_map(
        per_device,
        mesh=fine,
        in_specs=(both, P(COL), both, P(COL), both),
        out_specs=(both, both, both, P(COL), P(COL)),
        check_vma=False,
    )
```

```python
import math

import jax
import jax.numpy as jnp
from jax import lax
from jax.experimental import pallas as pl
from jax.experimental.pallas import tpu as pltpu
from jax.sharding import Mesh
from jax.sharding import PartitionSpec as P

D = 6144
PANEL = 768
BLOCK = 192
TOK = 256
Q = 64
VMEM = 60 * 2**20
AXES = ("x", "yl", "z", "yh", "k")
SIZES = (4, 2, 8, 2, 2)
ROW = ("x", "yl")
COL = ("z", "yh", "k")
QUAD = ("yh", "k")
f32, bf16 = jnp.float32, jnp.bfloat16


def gelu_parts(preact):
    coeff = math.sqrt(2.0 / math.pi)
    inner = coeff * (preact + 0.044715 * preact * preact * preact)
    tanh_val = jnp.tanh(inner)
    value = 0.5 * preact * (1.0 + tanh_val)
    slope = 0.5 * (1.0 + tanh_val) + 0.5 * preact * (1.0 - tanh_val * tanh_val) * coeff * (
        1.0 + 3.0 * 0.044715 * preact * preact
    )
    return (value, slope)


def shift(value, axis, by):
    size = SIZES[AXES.index(axis)]
    return lax.ppermute(value, axis, [(i, (i + by) % size) for i in range(size)])


def swap(value, m):
    return lax.ppermute(value, QUAD, [(i, i ^ m) for i in range(4)]) if m else value


def transpose(value):
    pairs = []
    for r in range(8):
        for z in range(8):
            for q in range(4):
                pairs.append((r * 32 + z * 4 + q, z * 32 + r * 4 + q))
    return lax.ppermute(value, AXES, pairs)


def to_all(value, axes, count):
    return lax.all_to_all(
        jnp.broadcast_to(value[None], (count,) + value.shape), axes, 0, 0
    )


def pick(stack, index):
    return lax.dynamic_index_in_dim(stack, index, 0, keepdims=False)


def trade(stack, q):
    got = jnp.stack([swap(pick(stack, q ^ m), m) for m in range(4)])
    return [pick(got, q ^ i) for i in range(4)]


def streamed(kernel, name, scalars, blocked, streams, out_shape, scratch):
    vmem = pl.BlockSpec(memory_space=pltpu.VMEM)
    return pl.pallas_call(
        kernel,
        in_specs=[pl.BlockSpec(memory_space=pltpu.SMEM)]
        + [vmem] * len(blocked)
        + [pl.BlockSpec(memory_space=pl.ANY)] * len(streams),
        out_specs=[vmem] * len(out_shape),
        out_shape=out_shape,
        scratch_shapes=scratch + [pltpu.SemaphoreType.DMA((len(streams),))],
        compiler_params=pltpu.CompilerParams(vmem_limit_bytes=VMEM),
        cost_estimate=pl.CostEstimate(flops=0, bytes_accessed=2**20, transcendentals=0),
        name=name,
    )(scalars, *blocked, *streams)


W_SCRATCH = pltpu.VMEM((4, PANEL, PANEL), bf16)
G_SCRATCH = pltpu.VMEM((8 * Q, 4 * PANEL), bf16)


def row_copies(s, first, rows, all_rows, sems):
    copies = []
    for i in range(8):
        at = pl.ds(pl.multiple_of(s[first + i] * Q, Q), Q)
        copies.append(pltpu.make_async_copy(rows[i], all_rows.at[at], sems.at[i]))
    return copies


def forward_kernel(s, gain, *refs):
    rows, ws, outs, (normed, held, parts, sems, out_sems) = (
        refs[:8], refs[8:12], refs[12:20], refs[20:]
    )
    copies = [pltpu.make_async_copy(w, held.at[i], sems.at[8 + i]) for i, w in enumerate(ws)]
    gathers = row_copies(s, 0, rows, normed, sems)
    for copy in gathers + copies:
        copy.start()
    normed[8 * Q :] = jnp.broadcast_to(gain[...], (16, PANEL))
    for copy in gathers:
        copy.wait()
    sums, sent = [], []
    for i in range(4):
        copies[i].wait()
        part = jnp.dot(normed[...], held[i], preferred_element_type=f32)
        parts[:, i * PANEL : (i + 1) * PANEL] = part[: 8 * Q].astype(bf16)
        one = part[8 * Q : 8 * Q + 1]
        sums += [one[:, j * 128 : (j + 1) * 128] for j in range(6)]
        stop = (i + 1) * PANEL
        if i == 3:
            extra = jnp.concatenate(sums + [jnp.zeros((Q - 24, 128), f32)], axis=0).astype(bf16)
            for j in range(8):
                parts[j * Q : (j + 1) * Q, stop:] = extra
            stop += 128
        columns = pl.ds(i * PANEL, stop - i * PANEL)
        for j in range(8):
            at = pl.ds(pl.multiple_of(s[8 + j] * Q, Q), Q)
            sent.append(
                pltpu.make_async_copy(
                    parts.at[at, columns], outs[j].at[:, columns], out_sems.at[8 * i + j]
                )
            )
            sent[-1].start()
    for copy in sent:
        copy.wait()


def forward(scalars, rows, gain, ws):
    wide = 4 * PANEL + 128
    hbm = pl.BlockSpec(memory_space=pl.ANY)
    vmem = pl.BlockSpec(memory_space=pltpu.VMEM)
    out = pl.pallas_call(
        forward_kernel,
        in_specs=[pl.BlockSpec(memory_space=pltpu.SMEM), vmem] + [hbm] * 12,
        out_specs=[hbm] * 8 + [vmem],
        out_shape=[jax.ShapeDtypeStruct((Q, wide), bf16)] * 8
        + [jax.ShapeDtypeStruct((8 * Q + 16, PANEL), bf16)],
        scratch_shapes=[
            W_SCRATCH,
            pltpu.VMEM((8 * Q, wide), bf16),
            pltpu.SemaphoreType.DMA((12,)),
            pltpu.SemaphoreType.DMA((32,)),
        ],
        compiler_params=pltpu.CompilerParams(vmem_limit_bytes=VMEM),
        cost_estimate=pl.CostEstimate(flops=0, bytes_accessed=2**20, transcendentals=0),
        name="forward",
    )(scalars, gain, *rows, *ws)
    return out[:8], out[8]


def backward_kernel(s, normed, pair, *refs):
    rows, ws, outs, (held, grads, blocks, sems, out_sems) = (
        refs[:8], refs[8:12], refs[12:20], refs[20:]
    )
    copies = row_copies(s, 8, rows, grads, sems)
    for i, w in enumerate(ws):
        copies.append(pltpu.make_async_copy(w, held.at[i], sems.at[8 + i]))
    for copy in copies:
        copy.start()
    for copy in copies[:8]:
        copy.wait()
    total = None
    for i in range(4):
        copies[8 + i].wait()
        part = lax.dot_general(
            grads[:, i * PANEL : (i + 1) * PANEL], held[i], (((1,), (1,)), ((), ())),
            preferred_element_type=f32,
        )
        total = part if total is None else total + part
    sums = jnp.sum(total * normed[: 8 * Q].astype(f32), axis=0, keepdims=True)
    extra = jnp.concatenate([pair[...], sums, jnp.zeros((14, PANEL), f32)], axis=0).astype(bf16)
    total = total.astype(bf16)
    for j in range(8):
        blocks[j, :Q] = total[j * Q : (j + 1) * Q]
        blocks[j, Q:] = extra
    sent = [pltpu.make_async_copy(blocks.at[s[j]], outs[j], out_sems.at[j]) for j in range(8)]
    for copy in sent:
        copy.start()
    for copy in sent:
        copy.wait()


def backward(scalars, grads, normed, pair, ws):
    hbm = pl.BlockSpec(memory_space=pl.ANY)
    vmem = pl.BlockSpec(memory_space=pltpu.VMEM)
    return pl.pallas_call(
        backward_kernel,
        in_specs=[pl.BlockSpec(memory_space=pltpu.SMEM), vmem, vmem] + [hbm] * 12,
        out_specs=[hbm] * 8,
        out_shape=[jax.ShapeDtypeStruct((Q + 16, PANEL), bf16)] * 8,
        scratch_shapes=[
            W_SCRATCH,
            G_SCRATCH,
            pltpu.VMEM((8, Q + 16, PANEL), bf16),
            pltpu.SemaphoreType.DMA((12,)),
            pltpu.SemaphoreType.DMA((8,)),
        ],
        compiler_params=pltpu.CompilerParams(vmem_limit_bytes=VMEM),
        cost_estimate=pl.CostEstimate(flops=0, bytes_accessed=2**20, transcendentals=0),
        name="backward",
    )(scalars, normed, pair, *grads, *ws)


def weight_kernel(s, normed, *refs):
    rows, (near, near_far, far, own, bias, grads, sems) = refs[:8], refs[8:]
    copies = row_copies(s, 8, rows, grads, sems)
    for copy in copies:
        copy.start()
    for copy in copies:
        copy.wait()
    for i, out in ((3, near_far), (1, far), (2, near), (0, own)):
        at = slice(i * PANEL, (i + 1) * PANEL)
        out[...] = lax.dot_general(
            normed[: 8 * Q], grads[:, at], (((0,), (0,)), ((), ())), preferred_element_type=f32
        ).astype(out.dtype)
    bias[...] = jnp.sum(grads[...].astype(f32), axis=0, keepdims=True)


def weight_products(scalars, normed, grads):
    shapes = [
        jax.ShapeDtypeStruct((PANEL, PANEL), bf16),
        jax.ShapeDtypeStruct((PANEL, PANEL), bf16),
        jax.ShapeDtypeStruct((PANEL, PANEL), f32),
        jax.ShapeDtypeStruct((PANEL, PANEL), f32),
        jax.ShapeDtypeStruct((1, 4 * PANEL), f32),
    ]
    return streamed(
        weight_kernel, "weight_products", scalars, [normed], grads, shapes, [G_SCRATCH]
    )


def add(a, b):
    return (a.astype(f32) + b.astype(f32)).astype(bf16)


def together(*values):
    return lax.optimization_barrier(values)


def per_device(activations, norm_gain, in_weight, in_bias, out_cotangent):
    row = lax.axis_index(ROW)
    z = lax.axis_index("z")
    q = lax.axis_index(QUAD)
    order = (0, 2, 1, 3)
    px, py = lax.axis_index("x"), lax.axis_index("yl")
    around = ((0, 0), (0, 1), (3, 0), (1, 0), (3, 1), (1, 1), (2, 0), (2, 1))
    scalars = jnp.stack([(px + a) % 4 * 2 + (py + b) % 2 for a, b in around]).astype(jnp.int32)

    x = jnp.concatenate(trade(activations.reshape(4, Q, BLOCK), q), axis=1)

    wide = activations.astype(f32)
    small = jnp.concatenate(
        [
            jnp.sum(wide, axis=1),
            jnp.sum(wide * wide, axis=1),
            norm_gain.astype(f32),
            jnp.zeros((64,), f32),
            in_bias,
            jnp.zeros((512,), f32),
        ]
    ).reshape(16, 128)
    smalls = to_all(small, COL, 32).reshape(32, 2048)
    cot = out_cotangent.reshape(4, Q, PANEL)
    cot = jnp.concatenate([swap(pick(cot, q ^ m), m) for m in order], axis=1)
    x, smalls, cot = together(x, smalls, cot)
    sums = jnp.sum(smalls[:, : 2 * TOK], axis=0).reshape(2, 4, Q, 1)
    sums = lax.dynamic_index_in_dim(sums, q, 1, keepdims=False)
    gains = smalls[:, 512:704]
    gain = lax.dynamic_slice(gains, (4 * z, 0), (4, BLOCK)).reshape(1, PANEL)
    average = sums[0] / D
    variance = sums[1] / D - average * average
    inv_std = lax.rsqrt(variance + 1e-06)
    x_hat = (x.astype(f32) - average) * inv_std
    normed = (x_hat * gain).astype(bf16)

    normed, weight = together(normed, in_weight)
    normed = transpose(normed)
    w_far, w_near = swap(weight, 2), swap(weight, 1)
    rows = {0: normed, 1: shift(normed, "z", 1), 7: shift(normed, "z", -1)}
    for i in (2, 3, 4):
        rows[i] = shift(rows[i - 1], "z", 1)
        if i < 4:
            rows[8 - i] = shift(rows[9 - i], "z", -1)
    w_far = together(w_far, rows[2], rows[6])[0]
    rows = [rows[i] for i in range(8)]
    places = jnp.stack([(z - i + 8) % 8 for i in range(8)]).astype(jnp.int32)
    scalars = jnp.concatenate([places, scalars])
    ws = (weight, w_far, w_near, swap(w_far, 1))
    gain_row = lax.dynamic_slice(gains, (4 * row, 0), (4, BLOCK)).reshape(1, PANEL).astype(bf16)
    rows, ws, gain_row = together(rows, ws, gain_row)
    blocks, normed = forward(scalars, rows, gain_row, ws)

    own, b01, b30, b10, b31, b11, b20, b21 = blocks
    got21, got11, got31 = shift(b21, "yl", 1), shift(b11, "x", 1), shift(b31, "yl", 1)
    b20, b01 = add(b20, got21), add(b01, got11)
    half_up, half_down = shift(b20[: Q // 2], "x", 1), shift(b20[Q // 2 :], "x", -1)
    got01 = shift(b01, "yl", 1)
    b10 = jnp.concatenate([add(b10[: Q // 2], half_up), b10[Q // 2 :]])
    b30 = add(b30, got31)
    b30 = jnp.concatenate([b30[: Q // 2], add(b30[Q // 2 :], half_down)])
    recv = (own, got01, shift(b10, "x", 1), shift(b30, "x", -1))
    biases = smalls[:, 768:1536]
    bias = jnp.concatenate([pick(biases, z * 4 + (q ^ m)) for m in order])
    recv, bias = together(recv, bias)
    total = sum(r.astype(f32) for r in recv)
    linear = total[:, : 4 * PANEL]
    value, slope = gelu_parts(linear + bias)
    hidden = value.astype(bf16)
    grad = (cot.astype(f32) * slope).astype(bf16)

    beside, below, above = shift(grad, "yl", 1), shift(grad, "x", 1), shift(grad, "x", -1)
    below_beside, above_beside = shift(beside, "x", 1), shift(above, "yl", 1)
    across = jnp.concatenate(
        [shift(below[: Q // 2], "x", 1), shift(above[Q // 2 :], "x", -1)], axis=0
    )
    across_beside = shift(across, "yl", 1)
    grads = [grad, beside, below, above, below_beside, above_beside, across, across_beside]
    wsum = total[:24, 4 * PANEL :].reshape(1, 4 * PANEL)
    pair = jnp.concatenate(
        [jnp.sum(grad.astype(f32) * wsum, axis=1), jnp.sum(grad.astype(f32) * linear, axis=1)]
    )
    pair = jnp.pad(pair[None], ((0, 0), (0, PANEL - 2 * Q)))
    grads, pair = together(grads, pair)

    back = backward(scalars, grads, normed, pair, ws)
    down, up = back[4], back[5]
    down, up, grads = together(down, up, grads)
    near, near_far, far, own, bias_total = weight_products(scalars, normed, grads)
    near_far = swap(near_far, 1)
    bias_near = bias_total[:, : 2 * PANEL] + swap(bias_total[:, 2 * PANEL :], 1)
    bias_far = swap(bias_near[:, PANEL:], 2)
    far = (far + near_far.astype(f32)).astype(bf16)
    far, bias_far = together(far, bias_far)
    far = swap(far, 2)
    near = swap(near, 1)
    for i in (3, 2, 1):
        down = add(shift(down, "z", -1), back[i])
        if i > 1:
            up = add(shift(up, "z", 1), back[9 - i])
    up, down = shift(up, "z", 1), shift(down, "z", -1)
    back = (up.astype(f32) + down.astype(f32) + back[0].astype(f32)).astype(bf16)
    back, far, hidden = together(back, far, hidden)
    pair = back[Q, : 2 * Q].astype(f32).reshape(2, Q, 1)
    back = transpose(back)
    got = [swap(hidden[:, i * PANEL : (i + 1) * PANEL], m) for i, m in enumerate(order)]
    got = jnp.stack([got[order.index(m)] for m in range(4)])
    hidden = jnp.concatenate([pick(got, q ^ i) for i in range(4)], axis=0)
    weight_grad = own + near.astype(f32) + far.astype(f32)
    back, weight_grad, hidden = together(back, weight_grad, hidden)
    scaled = back[:Q].astype(f32) * gain
    input_grad = (inv_std * (scaled - pair[0] / D - x_hat * (pair[1] / D))).astype(bf16)
    input_grad = jnp.concatenate([input_grad, back[Q:]])
    input_grad = jnp.stack([input_grad[:, i * BLOCK : (i + 1) * BLOCK] for i in range(4)])
    pieces = trade(input_grad, q)
    input_grad = jnp.concatenate([p[:Q] for p in pieces], axis=0)
    rows = sum(p[Q + 1].astype(f32) for p in pieces)
    gain_grad = rows / norm_gain.astype(f32)

    bias_grad = (bias_near[:, :PANEL] + bias_far)[0]
    return (hidden, input_grad, weight_grad, bias_grad, gain_grad)


def solution(mesh):
    fine = Mesh(mesh.devices.reshape(SIZES), AXES)
    both = P(ROW, COL)
    return jax.shard_map(
        per_device,
        mesh=fine,
        in_specs=(both, P(COL), both, P(COL), both),
        out_specs=(both, both, both, P(COL), P(COL)),
        check_vma=False,
    )
```

```python
import math

import jax
import jax.numpy as jnp
from jax import lax
from jax.experimental import pallas as pl
from jax.experimental.pallas import tpu as pltpu
from jax.sharding import Mesh
from jax.sharding import PartitionSpec as P

D = 6144
PANEL = 768
BLOCK = 192
TOK = 256
Q = 64
VMEM = 24 * 2**20
AXES = ("x", "yl", "z", "yh", "k")
SIZES = (4, 2, 8, 2, 2)
ROW = ("x", "yl")
COL = ("z", "yh", "k")
QUAD = ("yh", "k")
f32, bf16 = jnp.float32, jnp.bfloat16


def gelu_parts(preact):
    coeff = math.sqrt(2.0 / math.pi)
    inner = coeff * (preact + 0.044715 * preact * preact * preact)
    tanh_val = jnp.tanh(inner)
    value = 0.5 * preact * (1.0 + tanh_val)
    slope = 0.5 * (1.0 + tanh_val) + 0.5 * preact * (1.0 - tanh_val * tanh_val) * coeff * (
        1.0 + 3.0 * 0.044715 * preact * preact
    )
    return (value, slope)


def shift(value, axis, by):
    size = SIZES[AXES.index(axis)]
    return lax.ppermute(value, axis, [(i, (i + by) % size) for i in range(size)])


def swap(value, m):
    return lax.ppermute(value, QUAD, [(i, i ^ m) for i in range(4)]) if m else value


def transpose(value):
    pairs = []
    for r in range(8):
        for z in range(8):
            for q in range(4):
                pairs.append((r * 32 + z * 4 + q, z * 32 + r * 4 + q))
    return lax.ppermute(value, AXES, pairs)


def to_all(value, axes, count):
    return lax.all_to_all(
        jnp.broadcast_to(value[None], (count,) + value.shape), axes, 0, 0
    )


def pick(stack, index):
    return lax.dynamic_index_in_dim(stack, index, 0, keepdims=False)


def trade(stack, q):
    got = jnp.stack([swap(pick(stack, q ^ m), m) for m in range(4)])
    return [pick(got, q ^ i) for i in range(4)]


def streamed(kernel, name, scalars, blocked, streams, out_shape, scratch):
    vmem = pl.BlockSpec(memory_space=pltpu.VMEM)
    return pl.pallas_call(
        kernel,
        in_specs=[pl.BlockSpec(memory_space=pltpu.SMEM)]
        + [vmem] * len(blocked)
        + [pl.BlockSpec(memory_space=pl.ANY)] * len(streams),
        out_specs=[vmem] * len(out_shape),
        out_shape=out_shape,
        scratch_shapes=scratch + [pltpu.SemaphoreType.DMA((len(streams),))],
        compiler_params=pltpu.CompilerParams(vmem_limit_bytes=VMEM),
        cost_estimate=pl.CostEstimate(flops=0, bytes_accessed=2**20, transcendentals=0),
        name=name,
    )(scalars, *blocked, *streams)


W_SCRATCH = pltpu.VMEM((4, PANEL, PANEL), bf16)
G_SCRATCH = pltpu.VMEM((8 * Q, 4 * PANEL), bf16)


def row_copies(s, first, rows, all_rows, sems):
    copies = []
    for i in range(8):
        at = pl.ds(pl.multiple_of(s[first + i] * Q, Q), Q)
        copies.append(pltpu.make_async_copy(rows[i], all_rows.at[at], sems.at[i]))
    return copies


def forward_kernel(s, gain, *refs):
    rows, ws, outs, (normed, held, parts, sems, out_sems) = (
        refs[:8], refs[8:12], refs[12:20], refs[20:]
    )
    copies = [pltpu.make_async_copy(w, held.at[i], sems.at[8 + i]) for i, w in enumerate(ws)]
    gathers = row_copies(s, 0, rows, normed, sems)
    for copy in gathers + copies:
        copy.start()
    normed[8 * Q :] = jnp.broadcast_to(gain[...], (16, PANEL))
    for copy in gathers:
        copy.wait()
    sums, sent = [], []
    for i in range(4):
        copies[i].wait()
        part = jnp.dot(normed[...], held[i], preferred_element_type=f32)
        parts[:, i * PANEL : (i + 1) * PANEL] = part[: 8 * Q].astype(bf16)
        one = part[8 * Q : 8 * Q + 1]
        sums += [one[:, j * 128 : (j + 1) * 128] for j in range(6)]
        stop = (i + 1) * PANEL
        if i == 3:
            extra = jnp.concatenate(sums + [jnp.zeros((Q - 24, 128), f32)], axis=0).astype(bf16)
            for j in range(8):
                parts[j * Q : (j + 1) * Q, stop:] = extra
            stop += 128
        columns = pl.ds(i * PANEL, stop - i * PANEL)
        for j in range(8):
            at = pl.ds(pl.multiple_of(s[8 + j] * Q, Q), Q)
            sent.append(
                pltpu.make_async_copy(
                    parts.at[at, columns], outs[j].at[:, columns], out_sems.at[8 * i + j]
                )
            )
            sent[-1].start()
    for copy in sent:
        copy.wait()


def forward(scalars, rows, gain, ws):
    wide = 4 * PANEL + 128
    hbm = pl.BlockSpec(memory_space=pl.ANY)
    vmem = pl.BlockSpec(memory_space=pltpu.VMEM)
    out = pl.pallas_call(
        forward_kernel,
        in_specs=[pl.BlockSpec(memory_space=pltpu.SMEM), vmem] + [hbm] * 12,
        out_specs=[hbm] * 8 + [vmem],
        out_shape=[jax.ShapeDtypeStruct((Q, wide), bf16)] * 8
        + [jax.ShapeDtypeStruct((8 * Q + 16, PANEL), bf16)],
        scratch_shapes=[
            W_SCRATCH,
            pltpu.VMEM((8 * Q, wide), bf16),
            pltpu.SemaphoreType.DMA((12,)),
            pltpu.SemaphoreType.DMA((32,)),
        ],
        compiler_params=pltpu.CompilerParams(vmem_limit_bytes=VMEM),
        cost_estimate=pl.CostEstimate(flops=0, bytes_accessed=2**20, transcendentals=0),
        name="forward",
    )(scalars, gain, *rows, *ws)
    return out[:8], out[8]


def backward_kernel(s, normed, pair, *refs):
    rows, ws, outs, (held, grads, blocks, sems, out_sems) = (
        refs[:8], refs[8:12], refs[12:20], refs[20:]
    )
    copies = row_copies(s, 8, rows, grads, sems)
    for i, w in enumerate(ws):
        copies.append(pltpu.make_async_copy(w, held.at[i], sems.at[8 + i]))
    for copy in copies:
        copy.start()
    for copy in copies[:8]:
        copy.wait()
    total = None
    for i in range(4):
        copies[8 + i].wait()
        part = lax.dot_general(
            grads[:, i * PANEL : (i + 1) * PANEL], held[i], (((1,), (1,)), ((), ())),
            preferred_element_type=f32,
        )
        total = part if total is None else total + part
    sums = jnp.sum(total * normed[: 8 * Q].astype(f32), axis=0, keepdims=True)
    extra = jnp.concatenate([pair[...], sums, jnp.zeros((14, PANEL), f32)], axis=0).astype(bf16)
    total = total.astype(bf16)
    for j in range(8):
        blocks[j, :Q] = total[j * Q : (j + 1) * Q]
        blocks[j, Q:] = extra
    sent = [pltpu.make_async_copy(blocks.at[s[j]], outs[j], out_sems.at[j]) for j in range(8)]
    for copy in sent:
        copy.start()
    for copy in sent:
        copy.wait()


def backward(scalars, grads, normed, pair, ws):
    hbm = pl.BlockSpec(memory_space=pl.ANY)
    vmem = pl.BlockSpec(memory_space=pltpu.VMEM)
    return pl.pallas_call(
        backward_kernel,
        in_specs=[pl.BlockSpec(memory_space=pltpu.SMEM), vmem, vmem] + [hbm] * 12,
        out_specs=[hbm] * 8,
        out_shape=[jax.ShapeDtypeStruct((Q + 16, PANEL), bf16)] * 8,
        scratch_shapes=[
            W_SCRATCH,
            G_SCRATCH,
            pltpu.VMEM((8, Q + 16, PANEL), bf16),
            pltpu.SemaphoreType.DMA((12,)),
            pltpu.SemaphoreType.DMA((8,)),
        ],
        compiler_params=pltpu.CompilerParams(vmem_limit_bytes=VMEM),
        cost_estimate=pl.CostEstimate(flops=0, bytes_accessed=2**20, transcendentals=0),
        name="backward",
    )(scalars, normed, pair, *grads, *ws)


def weight_kernel(s, normed, *refs):
    rows, (near, near_far, far, own, bias, grads, sems) = refs[:8], refs[8:]
    copies = row_copies(s, 8, rows, grads, sems)
    for copy in copies:
        copy.start()
    for copy in copies:
        copy.wait()
    for i, out in ((3, near_far), (1, far), (2, near), (0, own)):
        at = slice(i * PANEL, (i + 1) * PANEL)
        out[...] = lax.dot_general(
            normed[: 8 * Q], grads[:, at], (((0,), (0,)), ((), ())), preferred_element_type=f32
        ).astype(out.dtype)
    bias[...] = jnp.sum(grads[...].astype(f32), axis=0, keepdims=True)


def weight_products(scalars, normed, grads):
    shapes = [
        jax.ShapeDtypeStruct((PANEL, PANEL), bf16),
        jax.ShapeDtypeStruct((PANEL, PANEL), bf16),
        jax.ShapeDtypeStruct((PANEL, PANEL), f32),
        jax.ShapeDtypeStruct((PANEL, PANEL), f32),
        jax.ShapeDtypeStruct((1, 4 * PANEL), f32),
    ]
    return streamed(
        weight_kernel, "weight_products", scalars, [normed], grads, shapes, [G_SCRATCH]
    )


def add(a, b):
    return (a.astype(f32) + b.astype(f32)).astype(bf16)


def together(*values):
    return lax.optimization_barrier(values)


def per_device(activations, norm_gain, in_weight, in_bias, out_cotangent):
    row = lax.axis_index(ROW)
    z = lax.axis_index("z")
    q = lax.axis_index(QUAD)
    order = (0, 2, 1, 3)
    px, py = lax.axis_index("x"), lax.axis_index("yl")
    around = ((0, 0), (0, 1), (3, 0), (1, 0), (3, 1), (1, 1), (2, 0), (2, 1))
    scalars = jnp.stack([(px + a) % 4 * 2 + (py + b) % 2 for a, b in around]).astype(jnp.int32)

    x = jnp.concatenate(trade(activations.reshape(4, Q, BLOCK), q), axis=1)

    wide = activations.astype(f32)
    small = jnp.concatenate(
        [
            jnp.sum(wide, axis=1),
            jnp.sum(wide * wide, axis=1),
            norm_gain.astype(f32),
            jnp.zeros((64,), f32),
            in_bias,
            jnp.zeros((512,), f32),
        ]
    ).reshape(16, 128)
    smalls = to_all(small, COL, 32).reshape(32, 2048)
    cot = out_cotangent.reshape(4, Q, PANEL)
    cot = jnp.concatenate([swap(pick(cot, q ^ m), m) for m in order], axis=1)
    x, smalls, cot = together(x, smalls, cot)
    sums = jnp.sum(smalls[:, : 2 * TOK], axis=0).reshape(2, 4, Q, 1)
    sums = lax.dynamic_index_in_dim(sums, q, 1, keepdims=False)
    gains = smalls[:, 512:704]
    gain = lax.dynamic_slice(gains, (4 * z, 0), (4, BLOCK)).reshape(1, PANEL)
    average = sums[0] / D
    variance = sums[1] / D - average * average
    inv_std = lax.rsqrt(variance + 1e-06)
    x_hat = (x.astype(f32) - average) * inv_std
    normed = (x_hat * gain).astype(bf16)

    normed, weight = together(normed, in_weight)
    normed = transpose(normed)
    w_far, w_near = swap(weight, 2), swap(weight, 1)
    rows = {0: normed, 1: shift(normed, "z", 1), 7: shift(normed, "z", -1)}
    for i in (2, 3, 4):
        rows[i] = shift(rows[i - 1], "z", 1)
        if i < 4:
            rows[8 - i] = shift(rows[9 - i], "z", -1)
    w_far = together(w_far, rows[2], rows[6])[0]
    rows = [rows[i] for i in range(8)]
    places = jnp.stack([(z - i + 8) % 8 for i in range(8)]).astype(jnp.int32)
    scalars = jnp.concatenate([places, scalars])
    ws = (weight, w_far, w_near, swap(w_far, 1))
    gain_row = lax.dynamic_slice(gains, (4 * row, 0), (4, BLOCK)).reshape(1, PANEL).astype(bf16)
    rows, ws, gain_row = together(rows, ws, gain_row)
    blocks, normed = forward(scalars, rows, gain_row, ws)

    own, b01, b30, b10, b31, b11, b20, b21 = blocks
    got21, got11, got31 = shift(b21, "yl", 1), shift(b11, "x", 1), shift(b31, "yl", 1)
    b20, b01 = add(b20, got21), add(b01, got11)
    half_up, half_down = shift(b20[: Q // 2], "x", 1), shift(b20[Q // 2 :], "x", -1)
    got01 = shift(b01, "yl", 1)
    b10 = jnp.concatenate([add(b10[: Q // 2], half_up), b10[Q // 2 :]])
    b30 = add(b30, got31)
    b30 = jnp.concatenate([b30[: Q // 2], add(b30[Q // 2 :], half_down)])
    recv = (own, got01, shift(b10, "x", 1), shift(b30, "x", -1))
    biases = smalls[:, 768:1536]
    bias = jnp.concatenate([pick(biases, z * 4 + (q ^ m)) for m in order])
    recv, bias = together(recv, bias)
    total = sum(r.astype(f32) for r in recv)
    linear = total[:, : 4 * PANEL]
    value, slope = gelu_parts(linear + bias)
    hidden = value.astype(bf16)
    grad = (cot.astype(f32) * slope).astype(bf16)

    beside, below, above = shift(grad, "yl", 1), shift(grad, "x", 1), shift(grad, "x", -1)
    below_beside, above_beside = shift(beside, "x", 1), shift(above, "yl", 1)
    across = jnp.concatenate(
        [shift(below[: Q // 2], "x", 1), shift(above[Q // 2 :], "x", -1)], axis=0
    )
    across_beside = shift(across, "yl", 1)
    grads = [grad, beside, below, above, below_beside, above_beside, across, across_beside]
    wsum = total[:24, 4 * PANEL :].reshape(1, 4 * PANEL)
    pair = jnp.concatenate(
        [jnp.sum(grad.astype(f32) * wsum, axis=1), jnp.sum(grad.astype(f32) * linear, axis=1)]
    )
    pair = jnp.pad(pair[None], ((0, 0), (0, PANEL - 2 * Q)))
    grads, pair = together(grads, pair)

    back = backward(scalars, grads, normed, pair, ws)
    down, up = back[4], back[5]
    down, up, grads = together(down, up, grads)
    near, near_far, far, own, bias_total = weight_products(scalars, normed, grads)
    near_far = swap(near_far, 1)
    bias_near = bias_total[:, : 2 * PANEL] + swap(bias_total[:, 2 * PANEL :], 1)
    bias_far = swap(bias_near[:, PANEL:], 2)
    far = (far + near_far.astype(f32)).astype(bf16)
    far, bias_far = together(far, bias_far)
    far = swap(far, 2)
    near = swap(near, 1)
    for i in (3, 2, 1):
        down = add(shift(down, "z", -1), back[i])
        if i > 1:
            up = add(shift(up, "z", 1), back[9 - i])
    up, down = shift(up, "z", 1), shift(down, "z", -1)
    back = (up.astype(f32) + down.astype(f32) + back[0].astype(f32)).astype(bf16)
    back, far, hidden = together(back, far, hidden)
    pair = back[Q, : 2 * Q].astype(f32).reshape(2, Q, 1)
    back = transpose(back)
    got = [swap(hidden[:, i * PANEL : (i + 1) * PANEL], m) for i, m in enumerate(order)]
    got = jnp.stack([got[order.index(m)] for m in range(4)])
    hidden = jnp.concatenate([pick(got, q ^ i) for i in range(4)], axis=0)
    weight_grad = own + near.astype(f32) + far.astype(f32)
    back, weight_grad, hidden = together(back, weight_grad, hidden)
    scaled = back[:Q].astype(f32) * gain
    input_grad = (inv_std * (scaled - pair[0] / D - x_hat * (pair[1] / D))).astype(bf16)
    input_grad = jnp.concatenate([input_grad, back[Q:]])
    input_grad = jnp.stack([input_grad[:, i * BLOCK : (i + 1) * BLOCK] for i in range(4)])
    pieces = trade(input_grad, q)
    input_grad = jnp.concatenate([p[:Q] for p in pieces], axis=0)
    rows = sum(p[Q + 1].astype(f32) for p in pieces)
    gain_grad = rows / norm_gain.astype(f32)

    bias_grad = (bias_near[:, :PANEL] + bias_far)[0]
    return (hidden, input_grad, weight_grad, bias_grad, gain_grad)


def solution(mesh):
    fine = Mesh(mesh.devices.reshape(SIZES), AXES)
    both = P(ROW, COL)
    return jax.shard_map(
        per_device,
        mesh=fine,
        in_specs=(both, P(COL), both, P(COL), both),
        out_specs=(both, both, both, P(COL), P(COL)),
        check_vma=False,
    )
```
